256 devices in a mesh: prow: 8 (over z), pcol: 32 (over x, y, core).
Axes of the slice: x: 4, y: 4, z: 8, core: 2. Of those that a mesh axis runs over, the one named last changes fastest.
Arguments:
- rhs: bfloat16 [4, 8, 32, 256, 128], P(None, 'prow', 'pcol'), may hold values from -6 to 6
- inverse_blocks: bfloat16 [4, 8, 32, 256, 256], P(None, 'prow', 'pcol'), may hold values from -1.5 to 1.5, as said below
- off_blocks: bfloat16 [3, 8, 32, 17, 256, 256], P(None, 'prow', 'pcol'), may hold values from -0.0625 to 0.0625
- targets: int32 [3, 8, 32, 17], P(None, 'prow', 'pcol'), may hold values from 8 to 31, as said below
Outputs:
- solution: bfloat16 [4, 8, 32, 256, 128], P(None, 'prow', 'pcol')
The draws below stay inside these ranges and needn't reach their ends.
Inputs may be any that keep to these rules, and one draw needn't show every extreme that they name: Every block of inverse_blocks is lower triangular with a positive diagonal. targets[h, r, c, j] names a block row on a level above h.
All inputs are finite; a program needn't handle non-finite values.
Results may differ from the reference program's by a relative error of at most 0.0056.
Values may be sent and summed in bfloat16 or wider, within the bound.
No kernel may reach another device: no remote copies, remote signals or barrier semaphores. Data moves between devices by JAX's collectives and lax.ppermute only.
A program may use at most 64 MiB of HBM per device.

```python
import math
import jax
import jax.numpy as jnp
from jax import lax

W = 256
NRHS = 128
LEV = 4
PROWS = 8
PCOLS = 32
NNZ = 17


def draw_inverse_blocks(key, part):
    key = jax.random.fold_in(key, 11)
    first_key, second_key = jax.random.split(key)
    shape = (LEV, PROWS, PCOLS, W, W)
    row_ids = lax.broadcasted_iota(jnp.int32, (W, W), 0)
    col_ids = lax.broadcasted_iota(jnp.int32, (W, W), 1)
    lower = (col_ids < row_ids).astype(jnp.float32)
    on_diagonal = (col_ids == row_ids).astype(jnp.float32)
    strict = jnp.clip(jax.random.normal(first_key, shape, jnp.float32), -3.0, 3.0)
    diagonal = jax.random.uniform(second_key, shape[:-1], jnp.float32, 0.5, 1.5)
    blocks = strict * lower / math.sqrt(W) + diagonal[..., :, None] * on_diagonal
    return blocks.astype(jnp.bfloat16)


def draw_targets(key, part):
    key = jax.random.fold_in(key, 23)
    first_key, second_key = jax.random.split(key)
    shape = (LEV - 1, PROWS, PCOLS, NNZ)
    height = lax.broadcasted_iota(jnp.int32, shape, 0)
    random_bits = jax.random.randint(first_key, shape, 0, 1 << 20)
    later = height + 1 + random_bits % (LEV - 1 - height)
    grid_row = jax.random.randint(second_key, shape, 0, PROWS)
    return (later * PROWS + grid_row).astype(jnp.int32)


def level_of(key, extent, cuts, low, largest):
    gain, own = 1.0, jax.random.fold_in(key, 6)
    for position, parts in cuts:
        steps = jnp.exp(jax.random.uniform(jax.random.fold_in(own, position), (parts,), jnp.float32, low / len(cuts), largest / len(cuts)))
        gain = gain * jnp.repeat(steps, extent[position] // parts).reshape([-1 if axis == position else 1 for axis in range(len(extent))])
    return gain


def scatter_about(key, dims, scale, reach, cuts=(), kind=jnp.bfloat16):
    drawn = jax.random.normal(key, dims, jnp.float32) * scale
    if len(cuts) > 0:
        drawn = level_of(key, dims, cuts, -0.22, 0.18) * drawn
    return jnp.clip(drawn, min=-reach, max=reach).astype(kind)


def setup_inputs(seed: int = 0) -> dict:
    keys = jax.random.split(jax.random.key(seed), 5)
    rhs = scatter_about(keys[0], (LEV, PROWS, PCOLS, W, NRHS), 1.0, 6.0, ((1, 8), (2, 32)))
    inverse_blocks = draw_inverse_blocks(jax.random.fold_in(keys[4], 71), 0)
    off_blocks = scatter_about(keys[2], (LEV - 1, PROWS, PCOLS, NNZ, W, W), (2 * W * NNZ) ** -0.5, 0.0625, ((1, 8), (2, 32)))
    targets = draw_targets(jax.random.fold_in(keys[4], 71), 0)
    return dict(rhs=rhs, inverse_blocks=inverse_blocks, off_blocks=off_blocks, targets=targets)


def reference(rhs, inverse_blocks, off_blocks, targets):
    pending = jnp.zeros((LEV * PROWS, PCOLS, W, NRHS), jnp.float32)
    col_index = (jnp.arange(PCOLS, dtype=jnp.int32)[:, None] - jnp.arange(NNZ, dtype=jnp.int32)[None, :]) % PCOLS
    col_owner = jnp.broadcast_to(jnp.arange(PCOLS, dtype=jnp.int32)[:, None], (PCOLS, NNZ))
    results = []
    for height in range(LEV):
        local_rhs = rhs[height].astype(jnp.float32) - pending[height * PROWS:(height + 1) * PROWS]
        residual = local_rhs.astype(jnp.bfloat16)
        solved = jnp.einsum("pqab,pqbr->pqar", inverse_blocks[height].astype(jnp.float32), residual.astype(jnp.float32), precision=lax.Precision.HIGHEST).astype(jnp.bfloat16)
        results.append(solved)
        if height + 1 < LEV:
            for grid_row in range(PROWS):
                pieces = solved[grid_row][col_index].astype(jnp.float32)
                products = jnp.einsum("cjab,cjbr->cjar", off_blocks[height, grid_row].astype(jnp.float32), pieces, precision=lax.Precision.HIGHEST)
                pending = pending.at[targets[height, grid_row], col_owner].add(products)
    return jnp.stack(results)
```

```python
import functools

import jax
import jax.numpy as jnp
from jax import lax
from jax.experimental import pallas as pl
from jax.experimental.pallas import tpu as pltpu
from jax.sharding import PartitionSpec as P

XS, YS, CORES = 4, 4, 2
VMEM_LIMIT = 16 * 1024 * 1024
F32, BF16 = jnp.float32, jnp.bfloat16

NEAR = (0, 4, 8)
FAR = (1, 5, 2, 6, 3, 7)


def vmem(n):
    return [pl.BlockSpec(memory_space=pltpu.VMEM)] * n


def smem():
    return pl.BlockSpec(memory_space=pltpu.SMEM)


def call(kernel, out_shape, in_specs, aliases=None, flops=0, nbytes=0, name=None):
    outs = len(out_shape) if isinstance(out_shape, (list, tuple)) else None
    return pl.pallas_call(
        kernel,
        out_shape=out_shape,
        in_specs=in_specs,
        out_specs=vmem(outs) if outs else vmem(1)[0],
        input_output_aliases=aliases or {},
        compiler_params=pltpu.CompilerParams(vmem_limit_bytes=VMEM_LIMIT),
        cost_estimate=pl.CostEstimate(flops=flops, bytes_accessed=nbytes, transcendentals=0),
        name=name,
    )


def first_solve_kernel(rhs_ref, inv_ref, out_ref):
    out_ref[...] = jnp.dot(inv_ref[...], rhs_ref[...], preferred_element_type=F32).astype(BF16)


def solve_kernel(parts_ref, rhs_ref, inv_ref, out_ref):
    total = parts_ref[0].astype(F32)
    for i in range(1, parts_ref.shape[0]):
        total = total + parts_ref[i].astype(F32)
    residual = (rhs_ref[...].astype(F32) - total).astype(BF16)
    out_ref[...] = jnp.dot(inv_ref[...], residual, preferred_element_type=F32).astype(BF16)


def add_product(tgt_ref, off_ref, acc_ref, j, piece, prows):
    row = tgt_ref[j] - prows
    product = jnp.dot(off_ref[j], piece, preferred_element_type=F32)
    acc_ref[row] = acc_ref[row] + product


def near_kernel(first, prows, core_ref, tgt_ref, off_ref, own_ref, sib_ref, *refs):
    acc_ref = refs[-1]
    if first:
        acc_ref[...] = jnp.zeros_like(acc_ref)
    core = core_ref[0]
    w = own_ref.shape[0] // 3
    for i, d in enumerate(NEAR):
        add_product(tgt_ref, off_ref, acc_ref, 2 * d, own_ref[i * w : (i + 1) * w], prows)
    for i in range(2):
        start = pl.multiple_of((i + 1 - core) * w, w)
        j = 8 * (i + 1 - core) - 1 + 2 * core
        add_product(tgt_ref, off_ref, acc_ref, j, sib_ref[pl.ds(start, w)], prows)


def mid_kernel(prows, tgt_ref, off_ref, p1_ref, p2_ref, p3_ref, acc_in, acc_ref):
    w = p1_ref.shape[0] // 2
    for s, ref in enumerate((p1_ref, p2_ref, p3_ref)):
        for half in range(2):
            d = FAR[2 * s + half]
            add_product(tgt_ref, off_ref, acc_ref, 2 * d, ref[half * w : (half + 1) * w], prows)


def late_kernel(
    base, prows, core_ref, tgt_ref, off_ref, p1_ref, p2_ref, p3_ref, acc_in, acc_ref, send_ref
):
    core = core_ref[0]
    w = p1_ref.shape[0] // 2
    for s, ref in enumerate((p1_ref, p2_ref, p3_ref)):
        for half in range(2):
            d = FAR[2 * s + half]
            j = 2 * d - 1 + 2 * core
            add_product(tgt_ref, off_ref, acc_ref, j, ref[half * w : (half + 1) * w], prows)
    for r in range(prows):
        send_ref[r] = acc_ref[base + r].astype(BF16)


def column_perm(move):
    pairs = []
    for x in range(XS):
        for y in range(YS):
            for k in range(CORES):
                a, b, c = move(x, y, k)
                pairs.append(((x * YS + y) * CORES + k, ((a % XS) * YS + b % YS) * CORES + c))
    return pairs


def shift_x(v, s):
    return lax.ppermute(v, "pcol", column_perm(lambda x, y, k: (x + s, y, k)))


def shift_y(v, s):
    return lax.ppermute(v, "pcol", column_perm(lambda x, y, k: (x, y + s, k)))


def sibling(v):
    return lax.ppermute(v, "pcol", column_perm(lambda x, y, k: (x, y, 1 - k)))


def local(rhs, inverse_blocks, off_blocks, targets):
    levels, width, cols = rhs.shape[0], rhs.shape[3], rhs.shape[4]
    band = off_blocks.shape[3]
    prows = lax.axis_size("prow")
    column = lax.axis_index("pcol")
    core = (column % CORES).astype(jnp.int32).reshape(1)
    y = (column // CORES) % YS
    rows = (levels - 1) * prows
    block = jax.ShapeDtypeStruct((width, cols), BF16)
    acc_shape = jax.ShapeDtypeStruct((rows, width, cols), F32)
    send_shape = jax.ShapeDtypeStruct((prows, width, cols), BF16)
    product_flops = 2 * width * width * cols
    acc = None
    results = []
    for h in range(levels):
        inv = inverse_blocks[h, 0, 0]
        if h == 0:
            solved = call(first_solve_kernel, block, vmem(2), flops=product_flops, name="solve0")(
                rhs[h, 0, 0], inv
            )
        else:
            solved = call(solve_kernel, block, vmem(3), flops=product_flops, name="solve")(
                parts, rhs[h, 0, 0], inv
            )
        results.append(solved)
        if h + 1 == levels:
            break
        off = off_blocks[h, 0, 0]
        tgt = targets[h, 0, 0]
        x1, x2 = shift_x(solved, 1), shift_x(solved, 2)
        near = jnp.concatenate([solved, x1, x2], axis=0)
        sib_near = sibling(near)
        far = []
        for s in (1, 2, 3):
            start = jnp.where(y + s >= YS, width, 0)
            far.append(shift_y(lax.dynamic_slice_in_dim(near, start, 2 * width, 0), s))
        sib_far = [sibling(v) for v in far]
        if h == 0:
            acc = call(
                functools.partial(near_kernel, True, prows),
                acc_shape,
                [smem(), smem()] + vmem(3),
                flops=5 * product_flops,
                name="near",
            )(core, tgt, off, near, sib_near)
        else:
            acc = call(
                functools.partial(near_kernel, False, prows),
                acc_shape,
                [smem(), smem()] + vmem(4),
                aliases={5: 0},
                flops=5 * product_flops,
                name="near",
            )(core, tgt, off, near, sib_near, acc)
        acc = call(
            functools.partial(mid_kernel, prows),
            acc_shape,
            [smem()] + vmem(5),
            aliases={5: 0},
            flops=6 * product_flops,
            name="mid",
        )(tgt, off, *far, acc)
        acc, send = call(
            functools.partial(late_kernel, h * prows, prows),
            (acc_shape, send_shape),
            [smem(), smem()] + vmem(5),
            aliases={6: 0},
            flops=6 * product_flops,
            name="late",
        )(core, tgt, off, *sib_far, acc)
        parts = lax.all_to_all(send, "prow", 0, 0, tiled=True)
    return jnp.stack(results)[:, None, None]


def solution(mesh):
    in_specs = (
        P(None, "prow", "pcol", None, None),
        P(None, "prow", "pcol", None, None),
        P(None, "prow", "pcol", None, None, None),
        P(None, "prow", "pcol", None),
    )
    out_specs = P(None, "prow", "pcol", None, None)
    return jax.shard_map(local, mesh=mesh, in_specs=in_specs, out_specs=out_specs, check_vma=False)
```

```python
import functools

import jax
import jax.numpy as jnp
from jax import lax
from jax.experimental import pallas as pl
from jax.experimental.pallas import tpu as pltpu
from jax.sharding import PartitionSpec as P

XS, YS, CORES = 4, 4, 2
VMEM_LIMIT = 16 * 1024 * 1024
F32, BF16 = jnp.float32, jnp.bfloat16

NEAR = (0, 4, 8)
SHIFTS = (1, 3, 2)


def spec(space):
    return pl.BlockSpec(memory_space=space)


def shape(*dims, dtype=BF16):
    return jax.ShapeDtypeStruct(dims, dtype)


def call(kernel, operands, outs, name, aliases=None, scratch=(), hbm=(), limit=VMEM_LIMIT, flops=0):
    single = not isinstance(outs, tuple)
    return pl.pallas_call(
        kernel,
        out_shape=outs,
        in_specs=[spec(pltpu.HBM if i in hbm else pltpu.VMEM) for i in range(len(operands))],
        out_specs=spec(pltpu.HBM if "out" in hbm else pltpu.VMEM)
        if single
        else tuple(spec(pltpu.VMEM) for _ in outs),
        scratch_shapes=list(scratch),
        input_output_aliases=aliases or {},
        compiler_params=pltpu.CompilerParams(vmem_limit_bytes=limit),
        cost_estimate=pl.CostEstimate(
            flops=flops or 500_000_000, bytes_accessed=1_500_000, transcendentals=0
        ),
        name=name,
    )(*operands)


def dot(a, b):
    return jnp.dot(a, b, preferred_element_type=F32)


def core_index():
    return lax.rem(lax.axis_index("pcol"), CORES)


def row_of(level, offset):
    prows = lax.axis_size("prow")
    sign = 1 - 2 * core_index()
    return level * prows + lax.rem(lax.axis_index("prow") + sign * offset + prows, prows)


def solved_block(level, acc_ref, up, down, two, minus, three, rhs_ref, inv_ref):
    w = rhs_ref.shape[1]
    total = acc_ref[row_of(level - 1, 0)]
    total = total + up[0:w].astype(F32) + down[0:w].astype(F32)
    for ref in (two, minus, three):
        total = total + ref[...].astype(F32)
    residual = (rhs_ref[level].astype(F32) - total).astype(BF16)
    return dot(inv_ref[level], residual).astype(BF16)


def solve_kernel(level, acc, up, down, two, minus, three, rhs, inv, out_ref):
    out_ref[...] = solved_block(level, acc, up, down, two, minus, three, rhs, inv)


def last_kernel(
    level, acc, up, down, two, minus, three, rhs, inv, s0, s1, s2, out_ref, last_v, sems
):
    copies = [
        pltpu.make_async_copy(ref, out_ref.at[i], sems.at[i]) for i, ref in enumerate((s0, s1, s2))
    ]
    for copy in copies:
        copy.start()
    last_v[...] = solved_block(level, acc, up, down, two, minus, three, rhs, inv)
    last = pltpu.make_async_copy(last_v, out_ref.at[level], sems.at[level])
    last.start()
    for copy in copies:
        copy.wait()
    last.wait()


def adder(level, tgt_ref, off_ref, acc_ref):
    prows = lax.axis_size("prow")

    def add(j, piece, other=None):
        row = tgt_ref[level, j]
        if other is not None:
            core = core_index()
            row = jnp.where(core == 0, row, tgt_ref[level, other])
            j = j + (other - j) * core
        row = row - prows
        acc_ref[row] = acc_ref[row] + dot(off_ref[level, j], piece)

    return add


def own_kernel(level, tgt_ref, off_ref, near_ref, *refs):
    acc_ref = refs[-1]
    fars = refs[: len(SHIFTS)]
    if level == 0:
        acc_ref[...] = jnp.zeros_like(acc_ref)
    add = adder(level, tgt_ref, off_ref, acc_ref)
    w = near_ref.shape[0] // 3
    for i, d in enumerate(NEAR):
        add(2 * d, near_ref[i * w : (i + 1) * w])
    for s, ref in zip(SHIFTS, fars):
        for half in range(2):
            add(2 * (s + 4 * half), ref[half * w : (half + 1) * w])


def late_kernel(
    level, tgt_ref, off_ref, sib_a, sib_b, sib_c, acc_in, acc_ref, up_ref, down_ref, two_ref
):
    add = adder(level, tgt_ref, off_ref, acc_ref)
    w = two_ref.shape[0]
    add(7, sib_a[0:w], 9)
    add(15, jnp.where(core_index() == 0, sib_c[0:w], sib_b[0:w]), 1)
    for s, ref in zip(SHIFTS, (sib_a, sib_b, sib_c)):
        for half in range(2):
            first = (1 + half) * w
            j = 2 * (s + 4 * half) - 1
            add(j, ref[first : first + w], j + 2)
    for ref, start, offset in (
        (up_ref, 0, 1),
        (up_ref, w, 4),
        (down_ref, 0, -1),
        (down_ref, w, -3),
        (two_ref, 0, 2),
    ):
        ref[start : start + w] = acc_ref[row_of(level, offset)].astype(BF16)


def merge_kernel(level, offset, acc_ref, got_ref, out_ref):
    w = out_ref.shape[0]
    total = acc_ref[row_of(level, offset)] + got_ref[w : 2 * w].astype(F32)
    out_ref[...] = total.astype(BF16)


def column_perm(move):
    pairs = []
    for x in range(XS):
        for y in range(YS):
            for k in range(CORES):
                a, b, c = move(x, y, k)
                pairs.append(((x * YS + y) * CORES + k, ((a % XS) * YS + b % YS) * CORES + c))
    return pairs


def shift_x(v, s):
    return lax.ppermute(v, "pcol", column_perm(lambda x, y, k: (x + s, y, k)))


def shift_y(v, s):
    return lax.ppermute(v, "pcol", column_perm(lambda x, y, k: (x, y + s, k)))


def sibling(v):
    return lax.ppermute(v, "pcol", column_perm(lambda x, y, k: (x, y, 1 - k)))


def shift_z(v, s, prows):
    cols = XS * YS * CORES
    pairs = [
        (r * cols + c, ((r + (s if c % CORES == 0 else -s)) % prows) * cols + c)
        for r in range(prows)
        for c in range(cols)
    ]
    return lax.ppermute(v, ("prow", "pcol"), pairs)


def local(rhs, inverse_blocks, off_blocks, targets):
    levels, width, cols = rhs.shape[0], rhs.shape[3], rhs.shape[4]
    prows = lax.axis_size("prow")
    y = (lax.axis_index("pcol") // CORES) % YS
    rhs = rhs.reshape(levels, width, cols)
    inv = inverse_blocks.reshape(levels, width, width)
    off = off_blocks.reshape(levels - 1, -1, width, width)
    tgt = targets.reshape(levels - 1, -1)
    block, pair = shape(width, cols), shape(2 * width, cols)
    acc_shape = shape((levels - 1) * prows, width, cols, dtype=F32)
    sums, results = (), []
    for h in range(levels):
        if h == 0:
            solved = dot(inv[0], rhs[0]).astype(BF16)
        elif h + 1 < levels:
            solved = call(functools.partial(solve_kernel, h), (*sums, rhs, inv), block, "solve")
        else:
            out = call(
                functools.partial(last_kernel, h),
                (*sums, rhs, inv, *results),
                shape(levels, width, cols),
                "last",
                hbm=("out",),
                scratch=[pltpu.VMEM((width, cols), BF16), pltpu.SemaphoreType.DMA((levels,))],
            )
            return out[:, None, None]
        results.append(solved)
        x1, x2 = shift_x(solved, 1), shift_x(solved, 2)
        blocks = off
        if h == 0:
            x1, x2, blocks = lax.optimization_barrier((x1, x2, off[:1]))
        near = jnp.concatenate([solved, x1, x2], axis=0)
        far = []
        for s in SHIFTS:
            start = jnp.where(y + s >= YS, width, 0)
            far.append(shift_y(lax.dynamic_slice_in_dim(near, start, 2 * width, 0), s))
        sibs = [sibling(jnp.concatenate([a, b], axis=0)) for a, b in zip((x1, solved, x2), far)]
        carried = () if h == 0 else (acc,)
        acc = call(
            functools.partial(own_kernel, h),
            (tgt, blocks, near, *far, *carried),
            acc_shape,
            "own",
            aliases={6: 0} if carried else None,
        )
        acc, up, down, two = call(
            functools.partial(late_kernel, h),
            (tgt, blocks, *sibs, acc),
            (acc_shape, pair, pair, block),
            "late",
            aliases={5: 0},
        )
        up, down, two = shift_z(up, 1, prows), shift_z(down, -1, prows), shift_z(two, 2, prows)
        merged = [
            shift_z(call(functools.partial(merge_kernel, h, offset), (acc, got), block, "merge"), offset, prows)
            for offset, got in ((-2, down), (3, up))
        ]
        sums = (acc, up, down, two, *merged)


def solution(mesh):
    in_specs = (
        P(None, "prow", "pcol", None, None),
        P(None, "prow", "pcol", None, None),
        P(None, "prow", "pcol", None, None, None),
        P(None, "prow", "pcol", None),
    )
    out_specs = P(None, "prow", "pcol", None, None)
    return jax.shard_map(local, mesh=mesh, in_specs=in_specs, out_specs=out_specs, check_vma=False)
```

```python
import functools

import jax
import jax.numpy as jnp
from jax import lax
from jax.experimental import pallas as pl
from jax.experimental.pallas import tpu as pltpu
from jax.sharding import PartitionSpec as P

XS, YS, CORES = 4, 4, 2
VMEM_LIMIT = 16 * 1024 * 1024
F32, BF16 = jnp.float32, jnp.bfloat16

NEAR = (0, 4, 8)
SHIFTS = (1, 3, 2)


def spec(space):
    return pl.BlockSpec(memory_space=space)


def shape(*dims, dtype=BF16):
    return jax.ShapeDtypeStruct(dims, dtype)


def call(kernel, operands, outs, name, aliases=None, scratch=(), hbm=(), limit=VMEM_LIMIT, flops=0):
    single = not isinstance(outs, tuple)
    return pl.pallas_call(
        kernel,
        out_shape=outs,
        in_specs=[spec(pltpu.HBM if i in hbm else pltpu.VMEM) for i in range(len(operands))],
        out_specs=spec(pltpu.HBM if "out" in hbm else pltpu.VMEM)
        if single
        else tuple(spec(pltpu.VMEM) for _ in outs),
        scratch_shapes=list(scratch),
        input_output_aliases=aliases or {},
        compiler_params=pltpu.CompilerParams(vmem_limit_bytes=limit),
        cost_estimate=pl.CostEstimate(
            flops=flops or 500_000_000, bytes_accessed=1_500_000, transcendentals=0
        ),
        name=name,
    )(*operands)


def dot(a, b):
    return jnp.dot(a, b, preferred_element_type=F32)


def core_index():
    return lax.rem(lax.axis_index("pcol"), CORES)


def row_of(level, offset):
    prows = lax.axis_size("prow")
    sign = 1 - 2 * core_index()
    return level * prows + lax.rem(lax.axis_index("prow") + sign * offset + prows, prows)


def solved_block(level, acc_ref, up, down, two, minus, three, rhs_ref, inv_ref):
    w = rhs_ref.shape[1]
    total = acc_ref[row_of(level - 1, 0)]
    total = total + up[0:w].astype(F32) + down[0:w].astype(F32)
    for ref in (two, minus, three):
        total = total + ref[...].astype(F32)
    residual = (rhs_ref[level].astype(F32) - total).astype(BF16)
    return dot(inv_ref[level], residual).astype(BF16)


def solve_kernel(level, acc, up, down, two, minus, three, rhs, inv, out_ref):
    out_ref[...] = solved_block(level, acc, up, down, two, minus, three, rhs, inv)


def last_kernel(
    level, acc, up, down, two, minus, three, rhs, inv, s0, s1, s2, out_ref, last_v, sems
):
    copies = [
        pltpu.make_async_copy(ref, out_ref.at[i], sems.at[i]) for i, ref in enumerate((s0, s1, s2))
    ]
    for copy in copies:
        copy.start()
    last_v[...] = solved_block(level, acc, up, down, two, minus, three, rhs, inv)
    last = pltpu.make_async_copy(last_v, out_ref.at[level], sems.at[level])
    last.start()
    for copy in copies:
        copy.wait()
    last.wait()


def adder(level, tgt_ref, off_ref, acc_ref):
    prows = lax.axis_size("prow")

    def add(j, piece, other=None):
        row = tgt_ref[level, j]
        if other is not None:
            core = core_index()
            row = jnp.where(core == 0, row, tgt_ref[level, other])
            j = j + (other - j) * core
        row = row - prows
        acc_ref[row] = acc_ref[row] + dot(off_ref[level, j], piece)

    return add


def own_kernel(level, tgt_ref, off_ref, near_ref, *refs):
    acc_ref = refs[-1]
    fars = refs[: len(SHIFTS)]
    if level == 0:
        acc_ref[...] = jnp.zeros_like(acc_ref)
    add = adder(level, tgt_ref, off_ref, acc_ref)
    w = near_ref.shape[0] // 3
    for i, d in enumerate(NEAR):
        add(2 * d, near_ref[i * w : (i + 1) * w])
    for s, ref in zip(SHIFTS, fars):
        for half in range(2):
            add(2 * (s + 4 * half), ref[half * w : (half + 1) * w])


def late_kernel(level, tgt_ref, off_ref, sib, acc_in, acc_ref, up_ref, down_ref, two_ref):
    add = adder(level, tgt_ref, off_ref, acc_ref)
    w = two_ref.shape[0]
    add(7, sib[w : 2 * w], 9)
    add(15, jnp.where(core_index() == 0, sib[2 * w : 3 * w], sib[0:w]), 1)
    for i, s in enumerate(SHIFTS):
        for half in range(2):
            first = (3 + 2 * i + half) * w
            j = 2 * (s + 4 * half) - 1
            add(j, sib[first : first + w], j + 2)
    for ref, start, offset in (
        (up_ref, 0, 1),
        (up_ref, w, 4),
        (down_ref, 0, -1),
        (down_ref, w, -3),
        (two_ref, 0, 2),
    ):
        ref[start : start + w] = acc_ref[row_of(level, offset)].astype(BF16)


def merge_kernel(level, offset, acc_ref, got_ref, out_ref):
    w = out_ref.shape[0]
    total = acc_ref[row_of(level, offset)] + got_ref[w : 2 * w].astype(F32)
    out_ref[...] = total.astype(BF16)


def column_perm(move):
    pairs = []
    for x in range(XS):
        for y in range(YS):
            for k in range(CORES):
                a, b, c = move(x, y, k)
                pairs.append(((x * YS + y) * CORES + k, ((a % XS) * YS + b % YS) * CORES + c))
    return pairs


def shift_x(v, s):
    return lax.ppermute(v, "pcol", column_perm(lambda x, y, k: (x + s, y, k)))


def shift_y(v, s):
    return lax.ppermute(v, "pcol", column_perm(lambda x, y, k: (x, y + s, k)))


def sibling(v):
    return lax.ppermute(v, "pcol", column_perm(lambda x, y, k: (x, y, 1 - k)))


def shift_z(v, s, prows):
    cols = XS * YS * CORES
    pairs = [
        (r * cols + c, ((r + (s if c % CORES == 0 else -s)) % prows) * cols + c)
        for r in range(prows)
        for c in range(cols)
    ]
    return lax.ppermute(v, ("prow", "pcol"), pairs)


def local(rhs, inverse_blocks, off_blocks, targets):
    levels, width, cols = rhs.shape[0], rhs.shape[3], rhs.shape[4]
    prows = lax.axis_size("prow")
    y = (lax.axis_index("pcol") // CORES) % YS
    rhs = rhs.reshape(levels, width, cols)
    inv = inverse_blocks.reshape(levels, width, width)
    off = off_blocks.reshape(levels - 1, -1, width, width)
    tgt = targets.reshape(levels - 1, -1)
    block, pair = shape(width, cols), shape(2 * width, cols)
    acc_shape = shape((levels - 1) * prows, width, cols, dtype=F32)
    sums, results = (), []
    for h in range(levels):
        if h == 0:
            solved = dot(inv[0], rhs[0]).astype(BF16)
        elif h + 1 < levels:
            solved = call(functools.partial(solve_kernel, h), (*sums, rhs, inv), block, "solve")
        else:
            out = call(
                functools.partial(last_kernel, h),
                (*sums, rhs, inv, *results),
                shape(levels, width, cols),
                "last",
                hbm=("out",),
                scratch=[pltpu.VMEM((width, cols), BF16), pltpu.SemaphoreType.DMA((levels,))],
            )
            return out[:, None, None]
        results.append(solved)
        x1, x2 = shift_x(solved, 1), shift_x(solved, 2)
        blocks = off
        if h == 0:
            x1, x2, blocks = lax.optimization_barrier((x1, x2, off[:1]))
        near = jnp.concatenate([solved, x1, x2], axis=0)
        far = []
        for s in SHIFTS:
            start = jnp.where(y + s >= YS, width, 0)
            far.append(shift_y(lax.dynamic_slice_in_dim(near, start, 2 * width, 0), s))
        sib = sibling(jnp.concatenate([near, *far], axis=0))
        carried = () if h == 0 else (acc,)
        acc = call(
            functools.partial(own_kernel, h),
            (tgt, blocks, near, *far, *carried),
            acc_shape,
            "own",
            aliases={6: 0} if carried else None,
        )
        acc, up, down, two = call(
            functools.partial(late_kernel, h),
            (tgt, blocks, sib, acc),
            (acc_shape, pair, pair, block),
            "late",
            aliases={3: 0},
        )
        up, down, two = shift_z(up, 1, prows), shift_z(down, -1, prows), shift_z(two, 2, prows)
        merged = [
            shift_z(call(functools.partial(merge_kernel, h, offset), (acc, got), block, "merge"), offset, prows)
            for offset, got in ((-2, down), (3, up))
        ]
        sums = (acc, up, down, two, *merged)


def solution(mesh):
    in_specs = (
        P(None, "prow", "pcol", None, None),
        P(None, "prow", "pcol", None, None),
        P(None, "prow", "pcol", None, None, None),
        P(None, "prow", "pcol", None),
    )
    out_specs = P(None, "prow", "pcol", None, None)
    return jax.shard_map(local, mesh=mesh, in_specs=in_specs, out_specs=out_specs, check_vma=False)
```

```python
import functools

import jax
import jax.numpy as jnp
from jax import lax
from jax.experimental import pallas as pl
from jax.experimental.pallas import tpu as pltpu
from jax.sharding import PartitionSpec as P

XS, YS, CORES = 4, 4, 2
VMEM_LIMIT = 16 * 1024 * 1024
F32, BF16 = jnp.float32, jnp.bfloat16

NEAR = (0, 4, 8)
SHIFTS = (1, 3, 2)


def spec(space):
    return pl.BlockSpec(memory_space=space)


def shape(*dims, dtype=BF16):
    return jax.ShapeDtypeStruct(dims, dtype)


def call(kernel, operands, outs, name, aliases=None, scratch=(), hbm=(), limit=VMEM_LIMIT, flops=0):
    single = not isinstance(outs, tuple)
    return pl.pallas_call(
        kernel,
        out_shape=outs,
        in_specs=[spec(pltpu.HBM if i in hbm else pltpu.VMEM) for i in range(len(operands))],
        out_specs=spec(pltpu.HBM if "out" in hbm else pltpu.VMEM)
        if single
        else tuple(spec(pltpu.VMEM) for _ in outs),
        scratch_shapes=list(scratch),
        input_output_aliases=aliases or {},
        compiler_params=pltpu.CompilerParams(vmem_limit_bytes=limit),
        cost_estimate=pl.CostEstimate(
            flops=flops or 500_000_000, bytes_accessed=1_500_000, transcendentals=0
        ),
        name=name,
    )(*operands)


def dot(a, b):
    return jnp.dot(a, b, preferred_element_type=F32)


def core_index():
    return lax.rem(lax.axis_index("pcol"), CORES)


def row_of(level, offset):
    prows = lax.axis_size("prow")
    sign = 1 - 2 * core_index()
    return level * prows + lax.rem(lax.axis_index("prow") + sign * offset + prows, prows)


def solved_block(level, acc_ref, up, down, two, minus, three, rhs_ref, inv_ref):
    w = rhs_ref.shape[1]
    total = acc_ref[row_of(level - 1, 0)]
    total = total + up[0:w].astype(F32) + down[0:w].astype(F32)
    for ref in (two, minus, three):
        total = total + ref[...].astype(F32)
    residual = (rhs_ref[level].astype(F32) - total).astype(BF16)
    return dot(inv_ref[level], residual).astype(BF16)


def solve_kernel(level, acc, up, down, two, minus, three, rhs, inv, out_ref):
    out_ref[...] = solved_block(level, acc, up, down, two, minus, three, rhs, inv)


def last_kernel(
    level, acc, up, down, two, minus, three, rhs, inv, s0, s1, s2, out_ref, last_v, sems
):
    copies = [
        pltpu.make_async_copy(ref, out_ref.at[i], sems.at[i]) for i, ref in enumerate((s0, s1, s2))
    ]
    for copy in copies:
        copy.start()
    last_v[...] = solved_block(level, acc, up, down, two, minus, three, rhs, inv)
    last = pltpu.make_async_copy(last_v, out_ref.at[level], sems.at[level])
    last.start()
    for copy in copies:
        copy.wait()
    last.wait()


def adder(level, tgt_ref, off_ref, acc_ref):
    prows = lax.axis_size("prow")

    def add(j, piece, other=None):
        row = tgt_ref[level, j]
        if other is not None:
            core = core_index()
            row = jnp.where(core == 0, row, tgt_ref[level, other])
            j = j + (other - j) * core
        row = row - prows
        acc_ref[row] = acc_ref[row] + dot(off_ref[level, j], piece)

    return add


def own_kernel(level, tgt_ref, off_ref, near_ref, *refs):
    acc_ref = refs[-1]
    fars = refs[: len(SHIFTS)]
    if level == 0:
        acc_ref[...] = jnp.zeros_like(acc_ref)
    add = adder(level, tgt_ref, off_ref, acc_ref)
    w = near_ref.shape[0] // 3
    for i, d in enumerate(NEAR):
        add(2 * d, near_ref[i * w : (i + 1) * w])
    for s, ref in zip(SHIFTS, fars):
        for half in range(2):
            add(2 * (s + 4 * half), ref[half * w : (half + 1) * w])


def late_kernel(level, tgt_ref, off_ref, sib, acc_in, acc_ref, up_ref, down_ref, two_ref):
    add = adder(level, tgt_ref, off_ref, acc_ref)
    w = two_ref.shape[0]
    add(7, sib[0:w], 1)
    add(15, sib[w : 2 * w], 9)
    for i, s in enumerate(SHIFTS):
        for half in range(2):
            first = (2 + 2 * i + half) * w
            j = 2 * (s + 4 * half) - 1
            add(j, sib[first : first + w], j + 2)
    for ref, start, offset in (
        (up_ref, 0, 1),
        (up_ref, w, 4),
        (down_ref, 0, -1),
        (down_ref, w, -3),
        (two_ref, 0, 2),
    ):
        ref[start : start + w] = acc_ref[row_of(level, offset)].astype(BF16)


def merge_kernel(level, offset, acc_ref, got_ref, out_ref):
    w = out_ref.shape[0]
    total = acc_ref[row_of(level, offset)] + got_ref[w : 2 * w].astype(F32)
    out_ref[...] = total.astype(BF16)


def column_perm(move):
    pairs = []
    for x in range(XS):
        for y in range(YS):
            for k in range(CORES):
                a, b, c = move(x, y, k)
                pairs.append(((x * YS + y) * CORES + k, ((a % XS) * YS + b % YS) * CORES + c))
    return pairs


def shift_x(v, s):
    return lax.ppermute(v, "pcol", column_perm(lambda x, y, k: (x + s, y, k)))


def shift_y(v, s):
    return lax.ppermute(v, "pcol", column_perm(lambda x, y, k: (x, y + s, k)))


def sibling(v):
    return lax.ppermute(v, "pcol", column_perm(lambda x, y, k: (x, y, 1 - k)))


def shift_z(v, s, prows):
    cols = XS * YS * CORES
    pairs = [
        (r * cols + c, ((r + (s if c % CORES == 0 else -s)) % prows) * cols + c)
        for r in range(prows)
        for c in range(cols)
    ]
    return lax.ppermute(v, ("prow", "pcol"), pairs)


def local(rhs, inverse_blocks, off_blocks, targets):
    levels, width, cols = rhs.shape[0], rhs.shape[3], rhs.shape[4]
    prows = lax.axis_size("prow")
    y = (lax.axis_index("pcol") // CORES) % YS
    core = lax.axis_index("pcol") % CORES
    rhs = rhs.reshape(levels, width, cols)
    inv = inverse_blocks.reshape(levels, width, width)
    off = off_blocks.reshape(levels - 1, -1, width, width)
    tgt = targets.reshape(levels - 1, -1)
    block, pair = shape(width, cols), shape(2 * width, cols)
    acc_shape = shape((levels - 1) * prows, width, cols, dtype=F32)
    sums, results = (), []
    for h in range(levels):
        if h == 0:
            solved = dot(inv[0], rhs[0]).astype(BF16)
        elif h + 1 < levels:
            solved = call(functools.partial(solve_kernel, h), (*sums, rhs, inv), block, "solve")
        else:
            out = call(
                functools.partial(last_kernel, h),
                (*sums, rhs, inv, *results),
                shape(levels, width, cols),
                "last",
                hbm=("out",),
                scratch=[pltpu.VMEM((width, cols), BF16), pltpu.SemaphoreType.DMA((levels,))],
            )
            return out[:, None, None]
        results.append(solved)
        x1, x2 = shift_x(solved, 1), shift_x(solved, 2)
        blocks = off
        if h == 0:
            x1, x2, blocks = lax.optimization_barrier((x1, x2, off[:1]))
        near = jnp.concatenate([solved, x1, x2], axis=0)
        far = []
        for s in SHIFTS:
            start = jnp.where(y + s >= YS, width, 0)
            far.append(shift_y(lax.dynamic_slice_in_dim(near, start, 2 * width, 0), s))
        needed = lax.dynamic_slice_in_dim(near, core * width, 2 * width, 0)
        sib = sibling(jnp.concatenate([needed, *far], axis=0))
        carried = () if h == 0 else (acc,)
        acc = call(
            functools.partial(own_kernel, h),
            (tgt, blocks, near, *far, *carried),
            acc_shape,
            "own",
            aliases={6: 0} if carried else None,
        )
        acc, up, down, two = call(
            functools.partial(late_kernel, h),
            (tgt, blocks, sib, acc),
            (acc_shape, pair, pair, block),
            "late",
            aliases={3: 0},
        )
        up, down, two = shift_z(up, 1, prows), shift_z(down, -1, prows), shift_z(two, 2, prows)
        merged = [
            shift_z(call(functools.partial(merge_kernel, h, offset), (acc, got), block, "merge"), offset, prows)
            for offset, got in ((-2, down), (3, up))
        ]
        sums = (acc, up, down, two, *merged)


def solution(mesh):
    in_specs = (
        P(None, "prow", "pcol", None, None),
        P(None, "prow", "pcol", None, None),
        P(None, "prow", "pcol", None, None, None),
        P(None, "prow", "pcol", None),
    )
    out_specs = P(None, "prow", "pcol", None, None)
    return jax.shard_map(local, mesh=mesh, in_specs=in_specs, out_specs=out_specs, check_vma=False)
```
